32 devices in a mesh: grp: 2 (over x), ha: 16 (over z, y, core).
Axes of the slice: x: 2, y: 2, z: 4, core: 2. Of those that a mesh axis runs over, the one named last changes fastest.
Arguments:
- frames: bfloat16 [4, 16, 112, 384], P('grp', 'ha'), parts along dimension 0, may hold values from -6 to 6
- cache_first: bfloat16 [4, 16, 112, 384], P('grp', 'ha'), parts along dimension 0, may hold values from -5 to 5
- cache_second: bfloat16 [4, 16, 112, 384], P('grp', 'ha'), parts along dimension 0, may hold values from -5 to 5
- gain_first: float32 [384], replicated, may hold values from 0.1 to 1.9
- gain_second: float32 [384], replicated, may hold values from 0.1 to 1.9
- bias_first: float32 [384], replicated, may hold values from -3 to 3
- bias_second: float32 [384], replicated, may hold values from -3 to 3
- weight_first: bfloat16 [10368, 384], P(None, 'ha'), may hold values from -0.0625 to 0.0625
- weight_second: bfloat16 [10368, 384], P(None, 'ha'), may hold values from -0.0625 to 0.0625
- cotangent: bfloat16 [4, 16, 112, 384], P('grp', 'ha'), parts along dimension 0, may hold values from -6 to 6
Outputs:
- output: bfloat16 [4, 16, 112, 384], P('grp', 'ha'), parts along dimension 0
- grad_frames: bfloat16 [4, 16, 112, 384], P('grp', 'ha'), parts along dimension 0
The draws below stay inside these ranges and needn't reach their ends.
There are 2 independent parts, one for each index of `grp`. The reference program is written for one: setup_inputs(seed, part) draws one part's arguments, and reference() takes and returns one part's arrays. A program takes and returns all parts, laid end to end along the dimension named above; an argument that names none is the same for every part. Nothing has to cross between parts.
All inputs are finite; a program needn't handle non-finite values.
Results may differ from the reference program's by a relative error of at most 0.006.
Values may be sent and summed in bfloat16 or wider, within the bound.
A program may use at most 128 MiB of HBM per device.

```python
import jax
import jax.numpy as jnp
from jax import lax

C = 384
FRAMES = 2
W = 112
H = 16


def level_of(own_key, extent, shards, low, largest):
    def one(axis_at, parts):
        heights = jax.random.uniform(jax.random.fold_in(jax.random.fold_in(own_key, 6), axis_at), (parts,), jnp.float32, low / len(shards), largest / len(shards))
        return jnp.repeat(jnp.exp(heights), extent[axis_at] // parts).reshape((-1,) + (1,) * (len(extent) - axis_at - 1))

    factor_of = one(*shards[0])
    for cut in shards[1:]:
        factor_of = factor_of * one(*cut)
    return factor_of


def noise(own_key, shape, deviation, limit, cuts=(), kind=jnp.bfloat16):
    array = jax.random.normal(own_key, shape, jnp.float32) * deviation
    if len(cuts) > 0:
        array = level_of(own_key, shape, cuts, -0.22, 0.18) * array
    return jnp.clip(array, min=-limit, max=limit).astype(kind)


def setup_inputs(seed: int = 0, part: int = 0) -> dict:
    seeds = jax.random.split(jax.random.key(seed), 11)
    part_splits = jax.random.split(jax.random.fold_in(seeds[10], part), 11)
    return {
        "frames": noise(part_splits[0], (FRAMES, H, W, C), 1.0, 6.0, ((1, 16),)),
        "cache_first": noise(part_splits[1], (2, H, W, C), 0.8, 5.0, ((1, 16),)),
        "cache_second": noise(part_splits[2], (2, H, W, C), 0.8, 5.0, ((1, 16),)),
        "gain_first": jnp.clip(1.0 + 0.18 * jax.random.normal(seeds[3], (C,), jnp.float32), 0.1, 1.9),
        "gain_second": jnp.clip(1.0 + 0.18 * jax.random.normal(seeds[4], (C,), jnp.float32), 0.1, 1.9),
        "bias_first": noise(seeds[5], (C,), 0.5, 3.0, (), jnp.float32),
        "bias_second": noise(seeds[6], (C,), 0.5, 3.0, (), jnp.float32),
        "weight_first": noise(seeds[7], (27 * C, C), (27 * C) ** -0.5, 0.0625, ((1, 16),)),
        "weight_second": noise(seeds[8], (27 * C, C), (27 * C) ** -0.5, 0.0625, ((1, 16),)),
        "cotangent": noise(part_splits[9], (FRAMES, H, W, C), 1.0, 6.0, ((1, 16),)),
    }


def normed_silu(values, scales):
    mean_square = lax.optimization_barrier(jnp.mean(values * values, axis=-1, keepdims=True))
    inverse = lax.rsqrt(mean_square + 1e-06)
    normed = values * inverse * scales
    return normed * jax.nn.sigmoid(normed)

def silu_backward(values, scales, upstream):
    mean_square = lax.optimization_barrier(jnp.mean(values * values, axis=-1, keepdims=True))
    inverse = lax.rsqrt(mean_square + 1e-06)
    normed = values * inverse * scales
    sigmoid_value = jax.nn.sigmoid(normed)
    scaled = scales * upstream * sigmoid_value * (1.0 + normed * (1.0 - sigmoid_value))
    return inverse * scaled - values * inverse ** 3 * lax.optimization_barrier(jnp.mean(values * scaled, axis=-1, keepdims=True))

def conv_forward(extended, weight):
    length = extended.shape[0] - 2
    height, columns, channels = (extended.shape[1], extended.shape[2], extended.shape[3])
    padded = jnp.pad(extended, ((0, 0), (1, 1), (1, 1), (0, 0)))
    kernel = weight.reshape(27, channels, channels)
    summed = jnp.zeros((length * height * columns, channels), jnp.float32)
    for frame_tap in range(3):
        for row_tap in range(3):
            for col_tap in range(3):
                window = padded[frame_tap:frame_tap + length, row_tap:row_tap + height, col_tap:col_tap + columns]
                summed = summed + jnp.dot(window.reshape(-1, channels), kernel[frame_tap * 9 + row_tap * 3 + col_tap], preferred_element_type=jnp.float32)
    return summed.reshape(length, height, columns, channels)

def conv_backward(upstream, weight):
    length, height, columns, channels = upstream.shape
    padded = jnp.pad(upstream, ((0, 2), (1, 1), (1, 1), (0, 0)))
    kernel = weight.reshape(27, channels, channels)
    summed = jnp.zeros((length * height * columns, channels), jnp.float32)
    for frame_tap in range(3):
        for row_tap in range(3):
            for col_tap in range(3):
                window = padded[2 - frame_tap:2 - frame_tap + length, 2 - row_tap:2 - row_tap + height, 2 - col_tap:2 - col_tap + columns]
                summed = summed + jnp.dot(window.reshape(-1, channels), kernel[frame_tap * 9 + row_tap * 3 + col_tap].T, preferred_element_type=jnp.float32)
    return summed.reshape(length, height, columns, channels)

def reference(frames, cache_first, cache_second, gain_first, gain_second, bias_first, bias_second, weight_first, weight_second, cotangent):
    inputs = frames.astype(jnp.float32)
    first_act = normed_silu(inputs, gain_first).astype(jnp.bfloat16)
    middle = (conv_forward(jnp.concatenate([cache_first, first_act], axis=0), weight_first) + bias_first).astype(jnp.bfloat16)
    middle_float = middle.astype(jnp.float32)
    second_act = normed_silu(middle_float, gain_second).astype(jnp.bfloat16)
    second_out = conv_forward(jnp.concatenate([cache_second, second_act], axis=0), weight_second) + bias_second
    output = (inputs + second_out).astype(jnp.bfloat16)
    grad_middle = silu_backward(middle_float, gain_second, conv_backward(cotangent, weight_second)).astype(jnp.bfloat16)
    grad_inputs = silu_backward(inputs, gain_first, conv_backward(grad_middle, weight_first))
    grad_frames = (cotangent.astype(jnp.float32) + grad_inputs).astype(jnp.bfloat16)
    return (output, grad_frames)
```

```python
import functools

import jax
import jax.numpy as jnp
from jax import lax
from jax.experimental import pallas as pl
from jax.experimental.pallas import tpu as pltpu
from jax.sharding import PartitionSpec as P


def extended_2(block, sides, width):
    for axis, dim in sides:
        count = lax.axis_size(axis)
        forward = [(i, i + 1) for i in range(count - 1)]
        backward = [(target, source) for source, target in forward]
        low = lax.ppermute(
            lax.slice_in_dim(block, block.shape[dim] - width, None, axis=dim), axis, forward
        )
        high = lax.ppermute(lax.slice_in_dim(block, 0, width, axis=dim), axis, backward)
        block = jnp.concatenate([low, block, high], axis=dim)
    return block


def normed_silu(values, scales):
    mean_square = jnp.mean(values * values, axis=-1, keepdims=True)
    inverse = lax.rsqrt(mean_square + 1e-06)
    normed = values * inverse * scales
    return normed * jax.nn.sigmoid(normed)


def silu_backward(values, scales, upstream):
    mean_square = jnp.mean(values * values, axis=-1, keepdims=True)
    inverse = lax.rsqrt(mean_square + 1e-06)
    normed = values * inverse * scales
    sigmoid_value = jax.nn.sigmoid(normed)
    scaled = scales * upstream * sigmoid_value * (1.0 + normed * (1.0 - sigmoid_value))
    return inverse * scaled - values * inverse**3 * jnp.mean(
        values * scaled, axis=-1, keepdims=True
    )


def tap_patches(padded, length, rows, columns, flipped):
    pieces = []
    for frame_tap in range(3):
        for row_tap in range(3):
            for col_tap in range(3):
                if flipped:
                    frame_start, row_start, col_start = (2 - frame_tap, 2 - row_tap, 2 - col_tap)
                else:
                    frame_start, row_start, col_start = (frame_tap, row_tap, col_tap)
                pieces.append(
                    padded[
                        frame_start : frame_start + length,
                        row_start : row_start + rows,
                        col_start : col_start + columns,
                    ]
                )
    return jnp.stack(pieces, axis=3)


def local_general(
    frames,
    cache_first,
    cache_second,
    gain_first,
    gain_second,
    bias_first,
    bias_second,
    weight_first,
    weight_second,
    cotangent,
):
    length, rows, columns, channels = frames.shape
    kernel_one, kernel_two = (
        lax.all_gather(weight_first, "ha", axis=1, tiled=True),
        lax.all_gather(weight_second, "ha", axis=1, tiled=True),
    )
    kernel_one = kernel_one.reshape(27, channels, channels)
    inputs = frames.astype(jnp.float32)
    first_act = normed_silu(inputs, gain_first).astype(jnp.bfloat16)
    extended = jnp.concatenate([cache_first, first_act], axis=0)
    padded = extended_2(extended, (("ha", 1),), 1)
    padded = jnp.pad(padded, ((0, 0), (0, 0), (1, 1), (0, 0)))
    patches = tap_patches(padded, length, rows, columns, False)
    middle = jnp.einsum("lrwtc,tco->lrwo", patches, kernel_one, preferred_element_type=jnp.float32)
    middle = (middle + bias_first).astype(jnp.bfloat16)
    middle_float = middle.astype(jnp.float32)
    kernel_two = kernel_two.reshape(27, channels, channels)
    second_act = normed_silu(middle_float, gain_second).astype(jnp.bfloat16)
    extended = jnp.concatenate([cache_second, second_act], axis=0)
    padded = extended_2(extended, (("ha", 1),), 1)
    padded = jnp.pad(padded, ((0, 0), (0, 0), (1, 1), (0, 0)))
    patches = tap_patches(padded, length, rows, columns, False)
    second_out = jnp.einsum(
        "lrwtc,tco->lrwo", patches, kernel_two, preferred_element_type=jnp.float32
    )
    output = (inputs + second_out + bias_second).astype(jnp.bfloat16)
    padded = extended_2(cotangent, (("ha", 1),), 1)
    padded = jnp.pad(padded, ((0, 2), (0, 0), (1, 1), (0, 0)))
    patches = tap_patches(padded, length, rows, columns, True)
    grad_second = jnp.einsum(
        "lrwto,tco->lrwc", patches, kernel_two, preferred_element_type=jnp.float32
    )
    grad_middle = silu_backward(middle_float, gain_second, grad_second).astype(jnp.bfloat16)
    padded = extended_2(grad_middle, (("ha", 1),), 1)
    padded = jnp.pad(padded, ((0, 2), (0, 0), (1, 1), (0, 0)))
    patches = tap_patches(padded, length, rows, columns, True)
    grad_first = jnp.einsum(
        "lrwto,tco->lrwc", patches, kernel_one, preferred_element_type=jnp.float32
    )
    grad_frames = (
        cotangent.astype(jnp.float32) + silu_backward(inputs, gain_first, grad_first)
    ).astype(jnp.bfloat16)
    return (output, grad_frames)


MESH = pl.DeviceIdType.MESH
LINE_AHEAD = 3


def block_kernel(
    n,
    groups,
    columns,
    frames_ref,
    cache_first_ref,
    cache_second_ref,
    gain_first_ref,
    gain_second_ref,
    bias_first_ref,
    bias_second_ref,
    cotangent_ref,
    shards,
    output_ref,
    grad_ref,
    buf,
    weights,
    early,
    act,
    grad_mid,
    patches_one,
    patches_two,
    acc,
    acc_t,
    middle_ref,
    z_send,
    z_recv,
    y_send,
    y_recv,
    x_send,
    x_recv,
    s_send,
    s_recv,
    t_send,
    t_recv,
    halo_send,
    halo_recv,
    local_sem,
):
    f32, bf16 = jnp.float32, jnp.bfloat16
    chunks, width, lanes = shards.shape
    half = chunks // 2
    channels = lanes // 3
    two = 2 * columns
    length = n // 4
    me = lax.axis_index("ha")
    group = lax.axis_index("grp")
    core = lax.rem(me, 2)
    row = lax.rem(me // 2, 2)
    line = me // 4
    odd = lax.rem(group, 2)
    own_off = pl.multiple_of(odd * channels, 128)
    give_off = pl.multiple_of(odd * 2 * channels, 128)
    take_off = pl.multiple_of((1 - odd) * 2 * channels, 128)

    def at(line_, row_, core_):
        return {"ha": (line_ * 2 + row_) * 2 + core_}

    sibling = at(line, row, 1 - core)
    across = at(line, 1 - row, core)
    twin = {"grp": group + 1 - 2 * odd}

    def line_peer(step):
        return at(lax.rem(line + step, length), row, core)

    barrier = pltpu.get_barrier_semaphore()
    partners = [sibling, across, twin] + [line_peer(s) for s in range(1, length)]
    for partner in partners:
        pl.semaphore_signal(barrier, inc=1, device_id=partner, device_id_type=MESH)

    has_low, has_high = me > 0, me < n - 1

    @pl.when(has_low)
    def _():
        pl.semaphore_signal(barrier, inc=1, device_id={"ha": me - 1}, device_id_type=MESH)

    @pl.when(has_high)
    def _():
        pl.semaphore_signal(barrier, inc=1, device_id={"ha": me + 1}, device_id_type=MESH)

    keep = pltpu.make_async_copy(
        shards.at[:, :, pl.ds(own_off, 2 * channels)],
        buf.at[:, core, row, line, :, pl.ds(own_off, 2 * channels)],
        local_sem,
    )
    keep.start()
    pl.semaphore_wait(
        barrier, len(partners) + has_low.astype(jnp.int32) + has_high.astype(jnp.int32)
    )

    def remote(src, dst, send, recv, device):
        return pltpu.make_async_remote_copy(
            src_ref=src, dst_ref=dst, send_sem=send, recv_sem=recv, device_id=device, device_id_type=MESH
        )

    def z_copy(q, step, source):
        return remote(
            shards.at[q, :, pl.ds(own_off, 2 * channels)],
            buf.at[q, core, row, source, :, pl.ds(own_off, 2 * channels)],
            z_send.at[q, step - 1],
            z_recv.at[q, step - 1],
            line_peer(step),
        )

    def same(view, send, recv, device):
        return remote(view, view, send, recv, device)

    def y_copy(q, row_):
        view = buf.at[q, core, row_, :, :, pl.ds(own_off, 2 * channels)]
        return same(view, y_send.at[q], y_recv.at[q], across)

    def x_copy(q, offset):
        view = buf.at[q, core, :, :, :, pl.ds(offset, channels)]
        return same(view, x_send.at[q], x_recv.at[q], twin)

    def s_copy(q, core_):
        view = buf.at[q, core_, :, :, :, pl.ds(own_off, 2 * channels)]
        return same(view, s_send.at[q], s_recv.at[q], sibling)

    def t_copy(q, core_):
        view = buf.at[q, core_, :, :, :, pl.ds(take_off, channels)]
        return same(view, t_send.at[q], t_recv.at[q], sibling)

    def z_start(q):
        for step in range(1, length):
            z_copy(q, step, line).start()

    def halo_copies(ref, index):
        low = remote(
            ref.at[1], ref.at[2], halo_send.at[index, 0], halo_recv.at[index, 0], {"ha": me - 1}
        )
        high = remote(
            ref.at[1], ref.at[0], halo_send.at[index, 1], halo_recv.at[index, 1], {"ha": me + 1}
        )
        return low, high

    def halo_start(ref, index):
        low, high = halo_copies(ref, index)

        @pl.when(has_low)
        def _():
            low.start()

        @pl.when(has_high)
        def _():
            high.start()

    def halo_wait(ref, index):
        low, high = halo_copies(ref, index)

        @pl.when(has_low)
        def _():
            high.wait_recv()
            low.wait_send()

        @pl.when(has_high)
        def _():
            low.wait_recv()
            high.wait_send()

        @pl.when(jnp.logical_not(has_low))
        def _():
            ref[0] = jnp.zeros(ref.shape[1:], ref.dtype)

        @pl.when(jnp.logical_not(has_high))
        def _():
            ref[2] = jnp.zeros(ref.shape[1:], ref.dtype)

    def comm(t):
        q = t + LINE_AHEAD + 4

        @pl.when(q < chunks)
        def _():
            z_start(q)

        q_z = t + 3

        @pl.when(q_z < chunks)
        def _():
            for step in range(1, length):
                z_copy(q_z, step, lax.rem(line - step + length, length)).wait_recv()
            y_copy(q_z, row).start()

        q_y = t + 2

        @pl.when(jnp.logical_and(q_y >= 0, q_y < chunks))
        def _():
            y_copy(q_y, 1 - row).wait_recv()
            x_copy(q_y, give_off).start()
            s_copy(q_y, core).start()

        q_x = t + 1

        @pl.when(jnp.logical_and(q_x >= 0, q_x < chunks))
        def _():
            x_copy(q_x, take_off).wait_recv()
            t_copy(q_x, core).start()

        @pl.when(t >= 0)
        def _():
            s_copy(t, 1 - core).wait_recv()
            t_copy(t, 1 - core).wait_recv()
            for index in range(n):
                weights[t, index * width : (index + 1) * width, :] = buf[
                    t, index % 2, index // 2 % 2, index // 4
                ]

    def column(shape):
        return lax.rem(lax.broadcasted_iota(jnp.int32, shape, 0), columns)

    def shifted(value, by):
        rolled = pltpu.roll(value, by % value.shape[0], 0)
        edge = 0 if by > 0 else columns - 1
        return jnp.where(column(value.shape) == edge, 0.0, rolled)

    def unfold(src, src_start, dst, dst_start, count):
        for j in range(3):
            value = src[j, src_start : src_start + count, :]
            wide = value.astype(f32)
            rows = slice(dst_start, dst_start + count)
            dst[j, rows, :channels] = shifted(wide, 1).astype(bf16)
            dst[j, rows, channels : 2 * channels] = value
            dst[j, rows, 2 * channels :] = shifted(wide, -1).astype(bf16)

    def forward_dot(patches, q, i, j):
        left = patches[j, pl.ds(pl.multiple_of(i * columns, 16), two), :]
        acc[...] += lax.dot_general(
            left, weights[q], (((1,), (1,)), ((), ())), preferred_element_type=f32
        )

    def back_late(ref, start, q, j):
        acc_t[...] += jnp.dot(
            ref[2 - j, start : start + two, :], weights[q], preferred_element_type=f32
        )

    def back_early(ref, start, q, j):
        acc_t[:columns, :] += jnp.dot(
            ref[2 - j, start + columns : start + two, :], weights[q], preferred_element_type=f32
        )

    def folded():
        return (
            shifted(acc_t[:, :channels], -1)
            + acc_t[:, channels : 2 * channels]
            + shifted(acc_t[:, 2 * channels :], 1)
        )

    for q in range(min(LINE_AHEAD + 1, chunks)):
        z_start(q)

    early[1, :two, :] = cache_first_ref[...]
    early[1, two : 2 * two, :] = normed_silu(frames_ref[...].astype(f32), gain_first_ref[...]).astype(bf16)
    early[1, 2 * two : 3 * two, :] = cache_second_ref[...]
    early[1, 3 * two :, :] = cotangent_ref[...]
    halo_start(early, 0)
    keep.wait()

    @pl.loop(-LINE_AHEAD, 0)
    def _(t):
        comm(t)

    halo_wait(early, 0)
    unfold(early, 0, patches_one, 0, 2 * two)
    unfold(early, 2 * two, patches_two, 0, two)
    acc[...] = jnp.zeros(acc.shape, f32)

    @pl.loop(0, half)
    def _(t):
        comm(t)
        forward_dot(patches_one, t, t // 3, lax.rem(t, 3))

    middle_ref[...] = (acc[...] + bias_first_ref[...]).astype(bf16)
    act[1] = normed_silu(middle_ref[...].astype(f32), gain_second_ref[...]).astype(bf16)
    halo_start(act, 1)
    acc[...] = jnp.zeros(acc.shape, f32)
    acc_t[...] = jnp.zeros(acc_t.shape, f32)
    comm(half)
    halo_wait(act, 1)
    unfold(act, 0, patches_two, two, two)

    @pl.loop(0, 3)
    def _(j):
        @pl.when(j > 0)
        def _():
            comm(half + j)

        back_late(early, 3 * two, half + j, j)
        forward_dot(patches_two, half + j, 2, j)

    @pl.loop(0, 3)
    def _(j):
        comm(half + 3 + j)
        back_early(early, 3 * two, half + 3 + j, j)
        forward_dot(patches_two, half + 3 + j, 1, j)

    grad_mid[1] = silu_backward(
        middle_ref[...].astype(f32), gain_second_ref[...], folded()
    ).astype(bf16)
    halo_start(grad_mid, 2)
    acc_t[...] = jnp.zeros(acc_t.shape, f32)
    comm(half + 6)
    forward_dot(patches_two, half + 6, 0, 0)
    halo_wait(grad_mid, 2)

    @pl.loop(0, 3)
    def _(j):
        back_late(grad_mid, 0, 6 + j, j)
        back_early(grad_mid, 0, 3 + j, j)

        @pl.when(j > 0)
        def _():
            comm(half + 6 + j)
            forward_dot(patches_two, half + 6 + j, 0, j)

    inputs = frames_ref[...].astype(f32)
    output_ref[...] = (inputs + acc[...] + bias_second_ref[...]).astype(bf16)
    grad_ref[...] = (
        cotangent_ref[...].astype(f32) + silu_backward(inputs, gain_first_ref[...], folded())
    ).astype(bf16)

    @pl.loop(0, chunks)
    def _(q):
        for step in range(1, length):
            z_copy(q, step, line).wait_send()
        y_copy(q, row).wait_send()
        x_copy(q, give_off).wait_send()
        s_copy(q, core).wait_send()
        t_copy(q, core).wait_send()


def local_fused(
    n,
    groups,
    frames,
    cache_first,
    cache_second,
    gain_first,
    gain_second,
    bias_first,
    bias_second,
    weight_first,
    weight_second,
    cotangent,
):
    _, _, columns, channels = frames.shape
    rows, width = weight_first.shape
    f32, bf16 = jnp.float32, jnp.bfloat16
    lanes = 3 * channels
    two = 2 * columns
    one = weight_first.T.reshape(width, 9, lanes).transpose(1, 0, 2)
    other = weight_second.T.reshape(width, 9, lanes).transpose(1, 0, 2)
    shards = jnp.concatenate([one, other[6:], other[3:6], other[:3]], axis=0)
    flat = lambda value: value.reshape(two, channels)
    vector = lambda value: value.reshape(1, channels)
    vmem = pl.BlockSpec(memory_space=pltpu.VMEM)
    dma = pltpu.SemaphoreType.DMA
    chunks, length = 18, n // 4
    outputs = pl.pallas_call(
        functools.partial(block_kernel, n, groups, columns),
        out_shape=[jax.ShapeDtypeStruct((two, channels), bf16)] * 2,
        in_specs=[vmem] * 9,
        out_specs=[vmem] * 2,
        scratch_shapes=[
            pltpu.VMEM((chunks, 2, 2, length, width, lanes), bf16),
            pltpu.VMEM((chunks, channels, lanes), bf16),
            pltpu.VMEM((3, 4 * two, channels), bf16),
            pltpu.VMEM((3, two, channels), bf16),
            pltpu.VMEM((3, two, channels), bf16),
            pltpu.VMEM((3, 2 * two, lanes), bf16),
            pltpu.VMEM((3, 2 * two, lanes), bf16),
            pltpu.VMEM((two, channels), f32),
            pltpu.VMEM((two, lanes), f32),
            pltpu.VMEM((two, channels), bf16),
            dma((chunks, length - 1)),
            dma((chunks, length - 1)),
            dma((chunks,)),
            dma((chunks,)),
            dma((chunks,)),
            dma((chunks,)),
            dma((chunks,)),
            dma((chunks,)),
            dma((chunks,)),
            dma((chunks,)),
            dma((3, 2)),
            dma((3, 2)),
            dma,
        ],
        compiler_params=pltpu.CompilerParams(
            collective_id=0, has_side_effects=True, vmem_limit_bytes=60 * 1024 * 1024
        ),
        cost_estimate=pl.CostEstimate(
            flops=6 * two * rows * channels, bytes_accessed=8 * rows * width, transcendentals=0
        ),
    )(
        flat(frames),
        flat(cache_first),
        flat(cache_second),
        vector(gain_first),
        vector(gain_second),
        vector(bias_first),
        vector(bias_second),
        flat(cotangent),
        shards,
    )
    return tuple(value.reshape(frames.shape) for value in outputs)


def local(n, groups, *arrays):
    frames, weight = arrays[0], arrays[7]
    fits = (
        n % 4 == 0
        and n >= 8
        and groups % 2 == 0
        and frames.shape[:2] == (2, 1)
        and frames.shape[2] % 16 == 0
        and frames.shape[3] % 128 == 0
        and weight.shape[1] % 8 == 0
    )
    if fits:
        return local_fused(n, groups, *arrays)
    return local_general(*arrays)


def solution(mesh):
    return jax.shard_map(
        functools.partial(local, mesh.shape["ha"], mesh.shape["grp"]),
        mesh=mesh,
        in_specs=(
            P("grp", "ha", None, None),
            P("grp", "ha", None, None),
            P("grp", "ha", None, None),
            P(),
            P(),
            P(),
            P(),
            P(None, "ha"),
            P(None, "ha"),
            P("grp", "ha", None, None),
        ),
        out_specs=(P("grp", "ha", None, None), P("grp", "ha", None, None)),
        check_vma=False,
    )
```

```python
import functools

import jax
import jax.numpy as jnp
from jax import lax
from jax.experimental import pallas as pl
from jax.experimental.pallas import tpu as pltpu
from jax.sharding import PartitionSpec as P


def extended_2(block, sides, width):
    for axis, dim in sides:
        count = lax.axis_size(axis)
        forward = [(i, i + 1) for i in range(count - 1)]
        backward = [(target, source) for source, target in forward]
        low = lax.ppermute(
            lax.slice_in_dim(block, block.shape[dim] - width, None, axis=dim), axis, forward
        )
        high = lax.ppermute(lax.slice_in_dim(block, 0, width, axis=dim), axis, backward)
        block = jnp.concatenate([low, block, high], axis=dim)
    return block


def normed_silu(values, scales):
    mean_square = jnp.mean(values * values, axis=-1, keepdims=True)
    inverse = lax.rsqrt(mean_square + 1e-06)
    normed = values * inverse * scales
    return normed * jax.nn.sigmoid(normed)


def silu_backward(values, scales, upstream):
    mean_square = jnp.mean(values * values, axis=-1, keepdims=True)
    inverse = lax.rsqrt(mean_square + 1e-06)
    normed = values * inverse * scales
    sigmoid_value = jax.nn.sigmoid(normed)
    scaled = scales * upstream * sigmoid_value * (1.0 + normed * (1.0 - sigmoid_value))
    return inverse * scaled - values * inverse**3 * jnp.mean(
        values * scaled, axis=-1, keepdims=True
    )


def tap_patches(padded, length, rows, columns, flipped):
    pieces = []
    for frame_tap in range(3):
        for row_tap in range(3):
            for col_tap in range(3):
                if flipped:
                    frame_start, row_start, col_start = (2 - frame_tap, 2 - row_tap, 2 - col_tap)
                else:
                    frame_start, row_start, col_start = (frame_tap, row_tap, col_tap)
                pieces.append(
                    padded[
                        frame_start : frame_start + length,
                        row_start : row_start + rows,
                        col_start : col_start + columns,
                    ]
                )
    return jnp.stack(pieces, axis=3)


def local_general(
    frames,
    cache_first,
    cache_second,
    gain_first,
    gain_second,
    bias_first,
    bias_second,
    weight_first,
    weight_second,
    cotangent,
):
    length, rows, columns, channels = frames.shape
    kernel_one, kernel_two = (
        lax.all_gather(weight_first, "ha", axis=1, tiled=True),
        lax.all_gather(weight_second, "ha", axis=1, tiled=True),
    )
    kernel_one = kernel_one.reshape(27, channels, channels)
    inputs = frames.astype(jnp.float32)
    first_act = normed_silu(inputs, gain_first).astype(jnp.bfloat16)
    extended = jnp.concatenate([cache_first, first_act], axis=0)
    padded = extended_2(extended, (("ha", 1),), 1)
    padded = jnp.pad(padded, ((0, 0), (0, 0), (1, 1), (0, 0)))
    patches = tap_patches(padded, length, rows, columns, False)
    middle = jnp.einsum("lrwtc,tco->lrwo", patches, kernel_one, preferred_element_type=jnp.float32)
    middle = (middle + bias_first).astype(jnp.bfloat16)
    middle_float = middle.astype(jnp.float32)
    kernel_two = kernel_two.reshape(27, channels, channels)
    second_act = normed_silu(middle_float, gain_second).astype(jnp.bfloat16)
    extended = jnp.concatenate([cache_second, second_act], axis=0)
    padded = extended_2(extended, (("ha", 1),), 1)
    padded = jnp.pad(padded, ((0, 0), (0, 0), (1, 1), (0, 0)))
    patches = tap_patches(padded, length, rows, columns, False)
    second_out = jnp.einsum(
        "lrwtc,tco->lrwo", patches, kernel_two, preferred_element_type=jnp.float32
    )
    output = (inputs + second_out + bias_second).astype(jnp.bfloat16)
    padded = extended_2(cotangent, (("ha", 1),), 1)
    padded = jnp.pad(padded, ((0, 2), (0, 0), (1, 1), (0, 0)))
    patches = tap_patches(padded, length, rows, columns, True)
    grad_second = jnp.einsum(
        "lrwto,tco->lrwc", patches, kernel_two, preferred_element_type=jnp.float32
    )
    grad_middle = silu_backward(middle_float, gain_second, grad_second).astype(jnp.bfloat16)
    padded = extended_2(grad_middle, (("ha", 1),), 1)
    padded = jnp.pad(padded, ((0, 2), (0, 0), (1, 1), (0, 0)))
    patches = tap_patches(padded, length, rows, columns, True)
    grad_first = jnp.einsum(
        "lrwto,tco->lrwc", patches, kernel_one, preferred_element_type=jnp.float32
    )
    grad_frames = (
        cotangent.astype(jnp.float32) + silu_backward(inputs, gain_first, grad_first)
    ).astype(jnp.bfloat16)
    return (output, grad_frames)


MESH = pl.DeviceIdType.MESH
DEPTH = 2
LINE_AHEAD = 3 * DEPTH


def block_kernel(
    n,
    groups,
    columns,
    frames_ref,
    cache_first_ref,
    cache_second_ref,
    gain_first_ref,
    gain_second_ref,
    bias_first_ref,
    bias_second_ref,
    cotangent_ref,
    shards,
    output_ref,
    grad_ref,
    buf,
    weights,
    early,
    act,
    grad_mid,
    patches_one,
    patches_two,
    acc,
    acc_t,
    middle_ref,
    z_send,
    z_recv,
    y_send,
    y_recv,
    x_send,
    x_recv,
    s_send,
    s_recv,
    t_send,
    t_recv,
    halo_send,
    halo_recv,
    local_sem,
):
    f32, bf16 = jnp.float32, jnp.bfloat16
    chunks, width, lanes = shards.shape
    half = chunks // 2
    channels = lanes // 3
    two = 2 * columns
    length = n // 4
    me = lax.axis_index("ha")
    group = lax.axis_index("grp")
    core = lax.rem(me, 2)
    row = lax.rem(me // 2, 2)
    line = me // 4
    odd = lax.rem(group, 2)
    own_off = pl.multiple_of(odd * channels, 128)
    give_off = pl.multiple_of(odd * 2 * channels, 128)
    take_off = pl.multiple_of((1 - odd) * 2 * channels, 128)

    def at(line_, row_, core_):
        return {"ha": (line_ * 2 + row_) * 2 + core_}

    sibling = at(line, row, 1 - core)
    across = at(line, 1 - row, core)
    twin = {"grp": group + 1 - 2 * odd}

    def line_peer(step):
        return at(lax.rem(line + step, length), row, core)

    barrier = pltpu.get_barrier_semaphore()
    partners = [sibling, across, twin] + [line_peer(s) for s in range(1, length)]
    for partner in partners:
        pl.semaphore_signal(barrier, inc=1, device_id=partner, device_id_type=MESH)

    has_low, has_high = me > 0, me < n - 1

    @pl.when(has_low)
    def _():
        pl.semaphore_signal(barrier, inc=1, device_id={"ha": me - 1}, device_id_type=MESH)

    @pl.when(has_high)
    def _():
        pl.semaphore_signal(barrier, inc=1, device_id={"ha": me + 1}, device_id_type=MESH)

    keep = pltpu.make_async_copy(
        shards.at[:, :, pl.ds(own_off, 2 * channels)],
        buf.at[:, core, row, line, :, pl.ds(own_off, 2 * channels)],
        local_sem,
    )
    keep.start()
    pl.semaphore_wait(
        barrier, len(partners) + has_low.astype(jnp.int32) + has_high.astype(jnp.int32)
    )

    def remote(src, dst, send, recv, device):
        return pltpu.make_async_remote_copy(
            src_ref=src, dst_ref=dst, send_sem=send, recv_sem=recv, device_id=device, device_id_type=MESH
        )

    def z_copy(q, step, source):
        return remote(
            shards.at[q, :, pl.ds(own_off, 2 * channels)],
            buf.at[q, core, row, source, :, pl.ds(own_off, 2 * channels)],
            z_send.at[q, step - 1],
            z_recv.at[q, step - 1],
            line_peer(step),
        )

    def same(view, send, recv, device):
        return remote(view, view, send, recv, device)

    def y_copy(q, row_):
        view = buf.at[q, core, row_, :, :, pl.ds(own_off, 2 * channels)]
        return same(view, y_send.at[q], y_recv.at[q], across)

    def x_copy(q, offset):
        view = buf.at[q, core, :, :, :, pl.ds(offset, channels)]
        return same(view, x_send.at[q], x_recv.at[q], twin)

    def s_copy(q, core_):
        view = buf.at[q, core_, :, :, :, pl.ds(own_off, 2 * channels)]
        return same(view, s_send.at[q], s_recv.at[q], sibling)

    def t_copy(q, core_):
        view = buf.at[q, core_, :, :, :, pl.ds(take_off, channels)]
        return same(view, t_send.at[q], t_recv.at[q], sibling)

    def z_start(q):
        for step in range(1, length):
            z_copy(q, step, line).start()

    def halo_copies(ref, index):
        low = remote(
            ref.at[1], ref.at[2], halo_send.at[index, 0], halo_recv.at[index, 0], {"ha": me - 1}
        )
        high = remote(
            ref.at[1], ref.at[0], halo_send.at[index, 1], halo_recv.at[index, 1], {"ha": me + 1}
        )
        return low, high

    def halo_start(ref, index):
        low, high = halo_copies(ref, index)

        @pl.when(has_low)
        def _():
            low.start()

        @pl.when(has_high)
        def _():
            high.start()

    def halo_wait(ref, index):
        low, high = halo_copies(ref, index)

        @pl.when(has_low)
        def _():
            high.wait_recv()
            low.wait_send()

        @pl.when(has_high)
        def _():
            low.wait_recv()
            high.wait_send()

        @pl.when(jnp.logical_not(has_low))
        def _():
            ref[0] = jnp.zeros(ref.shape[1:], ref.dtype)

        @pl.when(jnp.logical_not(has_high))
        def _():
            ref[2] = jnp.zeros(ref.shape[1:], ref.dtype)

    def comm(t):
        q = t + LINE_AHEAD + 4

        @pl.when(q < chunks)
        def _():
            z_start(q)

        q_z = t + LINE_AHEAD

        @pl.when(q_z < chunks)
        def _():
            for step in range(1, length):
                z_copy(q_z, step, lax.rem(line - step + length, length)).wait_recv()
            y_copy(q_z, row).start()

        q_y = t + 2 * DEPTH

        @pl.when(jnp.logical_and(q_y >= 0, q_y < chunks))
        def _():
            y_copy(q_y, 1 - row).wait_recv()
            x_copy(q_y, give_off).start()
            s_copy(q_y, core).start()

        q_x = t + DEPTH

        @pl.when(jnp.logical_and(q_x >= 0, q_x < chunks))
        def _():
            x_copy(q_x, take_off).wait_recv()
            t_copy(q_x, core).start()

        @pl.when(t >= 0)
        def _():
            s_copy(t, 1 - core).wait_recv()
            t_copy(t, 1 - core).wait_recv()
            for index in range(n):
                weights[t, index * width : (index + 1) * width, :] = buf[
                    t, index % 2, index // 2 % 2, index // 4
                ]

    def column(shape):
        return lax.rem(lax.broadcasted_iota(jnp.int32, shape, 0), columns)

    def shifted(value, by):
        rolled = pltpu.roll(value, by % value.shape[0], 0)
        edge = 0 if by > 0 else columns - 1
        return jnp.where(column(value.shape) == edge, 0.0, rolled)

    def unfold(src, src_start, dst, dst_start, count):
        for j in range(3):
            value = src[j, src_start : src_start + count, :]
            wide = value.astype(f32)
            rows = slice(dst_start, dst_start + count)
            dst[j, rows, :channels] = shifted(wide, 1).astype(bf16)
            dst[j, rows, channels : 2 * channels] = value
            dst[j, rows, 2 * channels :] = shifted(wide, -1).astype(bf16)

    def forward_dot(patches, q, i, j):
        left = patches[j, pl.ds(pl.multiple_of(i * columns, 16), two), :]
        acc[...] += lax.dot_general(
            left, weights[q], (((1,), (1,)), ((), ())), preferred_element_type=f32
        )

    def back_late(ref, start, q, j):
        acc_t[...] += jnp.dot(
            ref[2 - j, start : start + two, :], weights[q], preferred_element_type=f32
        )

    def back_early(ref, start, q, j):
        acc_t[:columns, :] += jnp.dot(
            ref[2 - j, start + columns : start + two, :], weights[q], preferred_element_type=f32
        )

    def folded():
        return (
            shifted(acc_t[:, :channels], -1)
            + acc_t[:, channels : 2 * channels]
            + shifted(acc_t[:, 2 * channels :], 1)
        )

    for q in range(min(4, chunks)):
        z_start(q)

    early[1, :two, :] = cache_first_ref[...]
    early[1, two : 2 * two, :] = normed_silu(frames_ref[...].astype(f32), gain_first_ref[...].reshape(1, channels)).astype(bf16)
    early[1, 2 * two : 3 * two, :] = cache_second_ref[...]
    early[1, 3 * two :, :] = cotangent_ref[...]
    halo_start(early, 0)
    keep.wait()

    @pl.loop(-LINE_AHEAD, 0)
    def _(t):
        comm(t)

    halo_wait(early, 0)
    unfold(early, 0, patches_one, 0, 2 * two)
    unfold(early, 2 * two, patches_two, 0, two)
    acc[...] = jnp.zeros(acc.shape, f32)

    @pl.loop(0, half)
    def _(t):
        comm(t)
        forward_dot(patches_one, t, t // 3, lax.rem(t, 3))

    middle_ref[...] = (acc[...] + bias_first_ref[...].reshape(1, channels)).astype(bf16)
    act[1] = normed_silu(middle_ref[...].astype(f32), gain_second_ref[...].reshape(1, channels)).astype(bf16)
    halo_start(act, 1)
    acc[...] = jnp.zeros(acc.shape, f32)
    acc_t[...] = jnp.zeros(acc_t.shape, f32)

    @pl.loop(0, 3)
    def _(j):
        comm(half + j)
        back_late(early, 3 * two, half + j, j)

    halo_wait(act, 1)
    unfold(act, 0, patches_two, two, two)

    @pl.loop(0, 3)
    def _(j):
        comm(half + 3 + j)
        back_early(early, 3 * two, half + 3 + j, j)
        forward_dot(patches_two, half + j, 2, j)
        forward_dot(patches_two, half + 3 + j, 1, j)

    grad_mid[1] = silu_backward(
        middle_ref[...].astype(f32), gain_second_ref[...].reshape(1, channels), folded()
    ).astype(bf16)
    halo_start(grad_mid, 2)
    acc_t[...] = jnp.zeros(acc_t.shape, f32)

    @pl.loop(0, 2)
    def _(j):
        comm(half + 6 + j)
        forward_dot(patches_two, half + 6 + j, 0, j)

    halo_wait(grad_mid, 2)

    @pl.loop(0, 3)
    def _(j):
        back_late(grad_mid, 0, 6 + j, j)
        back_early(grad_mid, 0, 3 + j, j)

    comm(half + 8)
    forward_dot(patches_two, half + 8, 0, 2)

    inputs = frames_ref[...].astype(f32)
    output_ref[...] = (inputs + acc[...] + bias_second_ref[...].reshape(1, channels)).astype(bf16)
    grad_ref[...] = (
        cotangent_ref[...].astype(f32) + silu_backward(inputs, gain_first_ref[...].reshape(1, channels), folded())
    ).astype(bf16)

    @pl.loop(0, chunks)
    def _(q):
        for step in range(1, length):
            z_copy(q, step, line).wait_send()
        y_copy(q, row).wait_send()
        x_copy(q, give_off).wait_send()
        s_copy(q, core).wait_send()
        t_copy(q, core).wait_send()


def local_fused(
    n,
    groups,
    frames,
    cache_first,
    cache_second,
    gain_first,
    gain_second,
    bias_first,
    bias_second,
    weight_first,
    weight_second,
    cotangent,
):
    _, _, columns, channels = frames.shape
    rows, width = weight_first.shape
    f32, bf16 = jnp.float32, jnp.bfloat16
    lanes = 3 * channels
    two = 2 * columns
    one = weight_first.T.reshape(width, 9, lanes).transpose(1, 0, 2)
    other = weight_second.T.reshape(width, 9, lanes).transpose(1, 0, 2)
    shards = jnp.concatenate([one, other[6:], other[3:6], other[:3]], axis=0)
    flat = lambda value: value.reshape(two, channels)
    vmem = pl.BlockSpec(memory_space=pltpu.VMEM)
    dma = pltpu.SemaphoreType.DMA
    chunks, length = 18, n // 4
    outputs = pl.pallas_call(
        functools.partial(block_kernel, n, groups, columns),
        out_shape=[jax.ShapeDtypeStruct((two, channels), bf16)] * 2,
        in_specs=[vmem] * 9,
        out_specs=[vmem] * 2,
        scratch_shapes=[
            pltpu.VMEM((chunks, 2, 2, length, width, lanes), bf16),
            pltpu.VMEM((chunks, channels, lanes), bf16),
            pltpu.VMEM((3, 4 * two, channels), bf16),
            pltpu.VMEM((3, two, channels), bf16),
            pltpu.VMEM((3, two, channels), bf16),
            pltpu.VMEM((3, 2 * two, lanes), bf16),
            pltpu.VMEM((3, 2 * two, lanes), bf16),
            pltpu.VMEM((two, channels), f32),
            pltpu.VMEM((two, lanes), f32),
            pltpu.VMEM((two, channels), bf16),
            dma((chunks, length - 1)),
            dma((chunks, length - 1)),
            dma((chunks,)),
            dma((chunks,)),
            dma((chunks,)),
            dma((chunks,)),
            dma((chunks,)),
            dma((chunks,)),
            dma((chunks,)),
            dma((chunks,)),
            dma((3, 2)),
            dma((3, 2)),
            dma,
        ],
        compiler_params=pltpu.CompilerParams(
            collective_id=0, has_side_effects=True, vmem_limit_bytes=60 * 1024 * 1024
        ),
        cost_estimate=pl.CostEstimate(
            flops=6 * two * rows * channels, bytes_accessed=8 * rows * width, transcendentals=0
        ),
    )(
        flat(frames),
        flat(cache_first),
        flat(cache_second),
        gain_first,
        gain_second,
        bias_first,
        bias_second,
        flat(cotangent),
        shards,
    )
    return tuple(value.reshape(frames.shape) for value in outputs)


def local(n, groups, *arrays):
    frames, weight = arrays[0], arrays[7]
    fits = (
        n % 4 == 0
        and n >= 8
        and groups % 2 == 0
        and frames.shape[:2] == (2, 1)
        and frames.shape[2] % 16 == 0
        and frames.shape[3] % 128 == 0
        and weight.shape[1] % 8 == 0
    )
    if fits:
        return local_fused(n, groups, *arrays)
    return local_general(*arrays)


def solution(mesh):
    return jax.shard_map(
        functools.partial(local, mesh.shape["ha"], mesh.shape["grp"]),
        mesh=mesh,
        in_specs=(
            P("grp", "ha", None, None),
            P("grp", "ha", None, None),
            P("grp", "ha", None, None),
            P(),
            P(),
            P(),
            P(),
            P(None, "ha"),
            P(None, "ha"),
            P("grp", "ha", None, None),
        ),
        out_specs=(P("grp", "ha", None, None), P("grp", "ha", None, None)),
        check_vma=False,
    )
```

```python
import functools

import jax
import jax.numpy as jnp
from jax import lax
from jax.experimental import pallas as pl
from jax.experimental.pallas import tpu as pltpu
from jax.sharding import PartitionSpec as P


def extended_2(block, sides, width):
    for axis, dim in sides:
        count = lax.axis_size(axis)
        forward = [(i, i + 1) for i in range(count - 1)]
        backward = [(target, source) for source, target in forward]
        low = lax.ppermute(
            lax.slice_in_dim(block, block.shape[dim] - width, None, axis=dim), axis, forward
        )
        high = lax.ppermute(lax.slice_in_dim(block, 0, width, axis=dim), axis, backward)
        block = jnp.concatenate([low, block, high], axis=dim)
    return block


def normed_silu(values, scales):
    mean_square = jnp.mean(values * values, axis=-1, keepdims=True)
    inverse = lax.rsqrt(mean_square + 1e-06)
    normed = values * inverse * scales
    return normed * jax.nn.sigmoid(normed)


def silu_backward(values, scales, upstream):
    mean_square = jnp.mean(values * values, axis=-1, keepdims=True)
    inverse = lax.rsqrt(mean_square + 1e-06)
    normed = values * inverse * scales
    sigmoid_value = jax.nn.sigmoid(normed)
    scaled = scales * upstream * sigmoid_value * (1.0 + normed * (1.0 - sigmoid_value))
    return inverse * scaled - values * inverse**3 * jnp.mean(
        values * scaled, axis=-1, keepdims=True
    )


def tap_patches(padded, length, rows, columns, flipped):
    pieces = []
    for frame_tap in range(3):
        for row_tap in range(3):
            for col_tap in range(3):
                if flipped:
                    frame_start, row_start, col_start = (2 - frame_tap, 2 - row_tap, 2 - col_tap)
                else:
                    frame_start, row_start, col_start = (frame_tap, row_tap, col_tap)
                pieces.append(
                    padded[
                        frame_start : frame_start + length,
                        row_start : row_start + rows,
                        col_start : col_start + columns,
                    ]
                )
    return jnp.stack(pieces, axis=3)


def local_general(
    frames,
    cache_first,
    cache_second,
    gain_first,
    gain_second,
    bias_first,
    bias_second,
    weight_first,
    weight_second,
    cotangent,
):
    length, rows, columns, channels = frames.shape
    kernel_one, kernel_two = (
        lax.all_gather(weight_first, "ha", axis=1, tiled=True),
        lax.all_gather(weight_second, "ha", axis=1, tiled=True),
    )
    kernel_one = kernel_one.reshape(27, channels, channels)
    inputs = frames.astype(jnp.float32)
    first_act = normed_silu(inputs, gain_first).astype(jnp.bfloat16)
    extended = jnp.concatenate([cache_first, first_act], axis=0)
    padded = extended_2(extended, (("ha", 1),), 1)
    padded = jnp.pad(padded, ((0, 0), (0, 0), (1, 1), (0, 0)))
    patches = tap_patches(padded, length, rows, columns, False)
    middle = jnp.einsum("lrwtc,tco->lrwo", patches, kernel_one, preferred_element_type=jnp.float32)
    middle = (middle + bias_first).astype(jnp.bfloat16)
    middle_float = middle.astype(jnp.float32)
    kernel_two = kernel_two.reshape(27, channels, channels)
    second_act = normed_silu(middle_float, gain_second).astype(jnp.bfloat16)
    extended = jnp.concatenate([cache_second, second_act], axis=0)
    padded = extended_2(extended, (("ha", 1),), 1)
    padded = jnp.pad(padded, ((0, 0), (0, 0), (1, 1), (0, 0)))
    patches = tap_patches(padded, length, rows, columns, False)
    second_out = jnp.einsum(
        "lrwtc,tco->lrwo", patches, kernel_two, preferred_element_type=jnp.float32
    )
    output = (inputs + second_out + bias_second).astype(jnp.bfloat16)
    padded = extended_2(cotangent, (("ha", 1),), 1)
    padded = jnp.pad(padded, ((0, 2), (0, 0), (1, 1), (0, 0)))
    patches = tap_patches(padded, length, rows, columns, True)
    grad_second = jnp.einsum(
        "lrwto,tco->lrwc", patches, kernel_two, preferred_element_type=jnp.float32
    )
    grad_middle = silu_backward(middle_float, gain_second, grad_second).astype(jnp.bfloat16)
    padded = extended_2(grad_middle, (("ha", 1),), 1)
    padded = jnp.pad(padded, ((0, 2), (0, 0), (1, 1), (0, 0)))
    patches = tap_patches(padded, length, rows, columns, True)
    grad_first = jnp.einsum(
        "lrwto,tco->lrwc", patches, kernel_one, preferred_element_type=jnp.float32
    )
    grad_frames = (
        cotangent.astype(jnp.float32) + silu_backward(inputs, gain_first, grad_first)
    ).astype(jnp.bfloat16)
    return (output, grad_frames)


MESH = pl.DeviceIdType.MESH
DEPTH = 2
LINE_AHEAD = 3 * DEPTH


def block_kernel(
    n,
    groups,
    columns,
    frames_ref,
    cache_first_ref,
    cache_second_ref,
    gain_first_ref,
    gain_second_ref,
    bias_first_ref,
    bias_second_ref,
    cotangent_ref,
    shards,
    output_ref,
    grad_ref,
    buf,
    weights,
    early,
    act,
    grad_mid,
    patches_one,
    patches_two,
    acc,
    acc_t,
    middle_ref,
    z_send,
    z_recv,
    y_send,
    y_recv,
    x_send,
    x_recv,
    s_send,
    s_recv,
    t_send,
    t_recv,
    halo_send,
    halo_recv,
    local_sem,
):
    f32, bf16 = jnp.float32, jnp.bfloat16
    chunks, tiles, width, _ = shards.shape
    half = chunks // 2
    lanes = tiles * 128
    channels = lanes // 3
    give = tiles // 2
    own = tiles - give
    two = 2 * columns
    length = n // 4
    me = lax.axis_index("ha")
    group = lax.axis_index("grp")
    core = lax.rem(me, 2)
    row = lax.rem(me // 2, 2)
    line = me // 4
    odd = lax.rem(group, 2)
    own_part = pl.ds(odd * give, own)
    give_part = pl.ds(odd * own, give)
    take_part = pl.ds((1 - odd) * own, give)

    def at(line_, row_, core_):
        return {"ha": (line_ * 2 + row_) * 2 + core_}

    sibling = at(line, row, 1 - core)
    across = at(line, 1 - row, core)
    twin = {"grp": group + 1 - 2 * odd}

    def line_peer(step):
        return at(lax.rem(line + step, length), row, core)

    barrier = pltpu.get_barrier_semaphore()
    partners = [sibling, across, twin] + [line_peer(s) for s in range(1, length)]
    for partner in partners:
        pl.semaphore_signal(barrier, inc=1, device_id=partner, device_id_type=MESH)

    has_low, has_high = me > 0, me < n - 1

    @pl.when(has_low)
    def _():
        pl.semaphore_signal(barrier, inc=1, device_id={"ha": me - 1}, device_id_type=MESH)

    @pl.when(has_high)
    def _():
        pl.semaphore_signal(barrier, inc=1, device_id={"ha": me + 1}, device_id_type=MESH)

    keep = pltpu.make_async_copy(
        shards,
        buf.at[:, core, row, line],
        local_sem,
    )
    keep.start()
    pl.semaphore_wait(
        barrier, len(partners) + has_low.astype(jnp.int32) + has_high.astype(jnp.int32)
    )

    def remote(src, dst, send, recv, device):
        return pltpu.make_async_remote_copy(
            src_ref=src, dst_ref=dst, send_sem=send, recv_sem=recv, device_id=device, device_id_type=MESH
        )

    def z_copy(q, step, source):
        return remote(
            shards.at[q, own_part],
            buf.at[q, core, row, source, own_part],
            z_send.at[q, step - 1],
            z_recv.at[q, step - 1],
            line_peer(step),
        )

    def same(view, send, recv, device):
        return remote(view, view, send, recv, device)

    def y_copy(q, row_):
        view = buf.at[q, core, row_, :, own_part]
        return same(view, y_send.at[q], y_recv.at[q], across)

    def x_one(q, step, part):
        source = lax.rem(line - step + length, length)
        view = buf.at[q, core, row, source, part]
        return same(view, x_send.at[q, step - 1], x_recv.at[q, step - 1], twin)

    def x_rest(q, part):
        view = buf.at[q, core, 1 - row, :, part]
        return same(view, x_send.at[q, length - 1], x_recv.at[q, length - 1], twin)

    def s_copy(q, core_):
        view = buf.at[q, core_, :, :, own_part]
        return same(view, s_send.at[q], s_recv.at[q], sibling)

    def t_copy(q, core_):
        view = buf.at[q, core_, :, :, take_part]
        return same(view, t_send.at[q], t_recv.at[q], sibling)

    def z_start(q):
        for step in range(1, length):
            z_copy(q, step, line).start()

    def halo_copies(ref, index):
        low = remote(
            ref.at[1], ref.at[2], halo_send.at[index, 0], halo_recv.at[index, 0], {"ha": me - 1}
        )
        high = remote(
            ref.at[1], ref.at[0], halo_send.at[index, 1], halo_recv.at[index, 1], {"ha": me + 1}
        )
        return low, high

    def halo_start(ref, index):
        low, high = halo_copies(ref, index)

        @pl.when(has_low)
        def _():
            low.start()

        @pl.when(has_high)
        def _():
            high.start()

    def halo_wait(ref, index):
        low, high = halo_copies(ref, index)

        @pl.when(has_low)
        def _():
            high.wait_recv()
            low.wait_send()

        @pl.when(has_high)
        def _():
            low.wait_recv()
            high.wait_send()

        @pl.when(jnp.logical_not(has_low))
        def _():
            ref[0] = jnp.zeros(ref.shape[1:], ref.dtype)

        @pl.when(jnp.logical_not(has_high))
        def _():
            ref[2] = jnp.zeros(ref.shape[1:], ref.dtype)

    def comm(t):
        q = t + LINE_AHEAD + 4

        @pl.when(q < chunks)
        def _():
            z_start(q)

        q_z = t + LINE_AHEAD

        @pl.when(q_z < chunks)
        def _():
            for step in range(1, length):
                z_copy(q_z, step, lax.rem(line - step + length, length)).wait_recv()
            y_copy(q_z, row).start()
            for step in range(1, length):
                x_one(q_z, step, give_part).start()

        q_y = t + 2 * DEPTH

        @pl.when(jnp.logical_and(q_y >= 0, q_y < chunks))
        def _():
            y_copy(q_y, 1 - row).wait_recv()
            x_rest(q_y, give_part).start()
            s_copy(q_y, core).start()

        q_x = t + DEPTH

        @pl.when(jnp.logical_and(q_x >= 0, q_x < chunks))
        def _():
            for step in range(1, length):
                x_one(q_x, step, take_part).wait_recv()
            x_rest(q_x, take_part).wait_recv()
            t_copy(q_x, core).start()

        @pl.when(t >= 0)
        def _():
            s_copy(t, 1 - core).wait_recv()
            t_copy(t, 1 - core).wait_recv()
            for index in range(n):
                rows = slice(index * width, (index + 1) * width)
                for m in range(tiles):
                    weights[t, rows, m * 128 : (m + 1) * 128] = buf[
                        t, index % 2, index // 2 % 2, index // 4, m
                    ]

    def column(shape):
        return lax.rem(lax.broadcasted_iota(jnp.int32, shape, 0), columns)

    def shifted(value, by):
        rolled = pltpu.roll(value, by % value.shape[0], 0)
        edge = 0 if by > 0 else columns - 1
        return jnp.where(column(value.shape) == edge, 0.0, rolled)

    def unfold(src, src_start, dst, dst_start, count):
        for j in range(3):
            value = src[j, src_start : src_start + count, :]
            wide = value.astype(f32)
            rows = slice(dst_start, dst_start + count)
            dst[j, rows, :channels] = shifted(wide, 1).astype(bf16)
            dst[j, rows, channels : 2 * channels] = value
            dst[j, rows, 2 * channels :] = shifted(wide, -1).astype(bf16)

    def forward_dot(patches, q, i, j):
        left = patches[j, pl.ds(pl.multiple_of(i * columns, 16), two), :]
        acc[...] += lax.dot_general(
            left, weights[q], (((1,), (1,)), ((), ())), preferred_element_type=f32
        )

    def back_late(ref, start, q, j):
        acc_t[...] += jnp.dot(
            ref[2 - j, start : start + two, :], weights[q], preferred_element_type=f32
        )

    def back_early(ref, start, q, j):
        acc_t[:columns, :] += jnp.dot(
            ref[2 - j, start + columns : start + two, :], weights[q], preferred_element_type=f32
        )

    def folded():
        return (
            shifted(acc_t[:, :channels], -1)
            + acc_t[:, channels : 2 * channels]
            + shifted(acc_t[:, 2 * channels :], 1)
        )

    for q in range(min(4, chunks)):
        z_start(q)

    early[1, :two, :] = cache_first_ref[...]
    early[1, two : 2 * two, :] = normed_silu(frames_ref[...].astype(f32), gain_first_ref[...].reshape(1, channels)).astype(bf16)
    early[1, 2 * two : 3 * two, :] = cache_second_ref[...]
    early[1, 3 * two :, :] = cotangent_ref[...]
    halo_start(early, 0)
    keep.wait()

    @pl.loop(-LINE_AHEAD, 0)
    def _(t):
        comm(t)

    halo_wait(early, 0)
    unfold(early, 0, patches_one, 0, 2 * two)
    unfold(early, 2 * two, patches_two, 0, two)
    acc[...] = jnp.zeros(acc.shape, f32)

    @pl.loop(0, half)
    def _(t):
        comm(t)
        forward_dot(patches_one, t, t // 3, lax.rem(t, 3))

    middle_ref[...] = (acc[...] + bias_first_ref[...].reshape(1, channels)).astype(bf16)
    act[1] = normed_silu(middle_ref[...].astype(f32), gain_second_ref[...].reshape(1, channels)).astype(bf16)
    halo_start(act, 1)
    acc[...] = jnp.zeros(acc.shape, f32)
    acc_t[...] = jnp.zeros(acc_t.shape, f32)

    @pl.loop(0, 3)
    def _(j):
        comm(half + j)
        back_late(early, 3 * two, half + j, j)

    halo_wait(act, 1)
    unfold(act, 0, patches_two, two, two)

    @pl.loop(0, 3)
    def _(j):
        comm(half + 3 + j)
        back_early(early, 3 * two, half + 3 + j, j)
        forward_dot(patches_two, half + j, 2, j)
        forward_dot(patches_two, half + 3 + j, 1, j)

    grad_mid[1] = silu_backward(
        middle_ref[...].astype(f32), gain_second_ref[...].reshape(1, channels), folded()
    ).astype(bf16)
    halo_start(grad_mid, 2)
    acc_t[...] = jnp.zeros(acc_t.shape, f32)

    @pl.loop(0, 2)
    def _(j):
        comm(half + 6 + j)
        forward_dot(patches_two, half + 6 + j, 0, j)

    halo_wait(grad_mid, 2)

    @pl.loop(0, 3)
    def _(j):
        back_late(grad_mid, 0, 6 + j, j)
        back_early(grad_mid, 0, 3 + j, j)

    comm(half + 8)
    forward_dot(patches_two, half + 8, 0, 2)

    inputs = frames_ref[...].astype(f32)
    output_ref[...] = (inputs + acc[...] + bias_second_ref[...].reshape(1, channels)).astype(bf16)
    grad_ref[...] = (
        cotangent_ref[...].astype(f32) + silu_backward(inputs, gain_first_ref[...].reshape(1, channels), folded())
    ).astype(bf16)

    @pl.loop(0, chunks)
    def _(q):
        for step in range(1, length):
            z_copy(q, step, line).wait_send()
            x_one(q, step, give_part).wait_send()
        y_copy(q, row).wait_send()
        x_rest(q, give_part).wait_send()
        s_copy(q, core).wait_send()
        t_copy(q, core).wait_send()


def local_fused(
    n,
    groups,
    frames,
    cache_first,
    cache_second,
    gain_first,
    gain_second,
    bias_first,
    bias_second,
    weight_first,
    weight_second,
    cotangent,
):
    _, _, columns, channels = frames.shape
    rows, width = weight_first.shape
    f32, bf16 = jnp.float32, jnp.bfloat16
    lanes = 3 * channels
    two = 2 * columns
    tiles = lanes // 128
    one = weight_first.T.reshape(width, 9, tiles, 128).transpose(1, 2, 0, 3)
    other = weight_second.T.reshape(width, 9, tiles, 128).transpose(1, 2, 0, 3)
    shards = jnp.concatenate([one, other[6:], other[3:6], other[:3]], axis=0)
    flat = lambda value: value.reshape(two, channels)
    vmem = pl.BlockSpec(memory_space=pltpu.VMEM)
    dma = pltpu.SemaphoreType.DMA
    chunks, length = 18, n // 4
    outputs = pl.pallas_call(
        functools.partial(block_kernel, n, groups, columns),
        out_shape=[jax.ShapeDtypeStruct((two, channels), bf16)] * 2,
        in_specs=[vmem] * 9,
        out_specs=[vmem] * 2,
        scratch_shapes=[
            pltpu.VMEM((chunks, 2, 2, length, tiles, width, 128), bf16),
            pltpu.VMEM((chunks, channels, lanes), bf16),
            pltpu.VMEM((3, 4 * two, channels), bf16),
            pltpu.VMEM((3, two, channels), bf16),
            pltpu.VMEM((3, two, channels), bf16),
            pltpu.VMEM((3, 2 * two, lanes), bf16),
            pltpu.VMEM((3, 2 * two, lanes), bf16),
            pltpu.VMEM((two, channels), f32),
            pltpu.VMEM((two, lanes), f32),
            pltpu.VMEM((two, channels), bf16),
            dma((chunks, length - 1)),
            dma((chunks, length - 1)),
            dma((chunks,)),
            dma((chunks,)),
            dma((chunks, length)),
            dma((chunks, length)),
            dma((chunks,)),
            dma((chunks,)),
            dma((chunks,)),
            dma((chunks,)),
            dma((3, 2)),
            dma((3, 2)),
            dma,
        ],
        compiler_params=pltpu.CompilerParams(
            collective_id=0, has_side_effects=True, vmem_limit_bytes=60 * 1024 * 1024
        ),
        cost_estimate=pl.CostEstimate(
            flops=6 * two * rows * channels, bytes_accessed=8 * rows * width, transcendentals=0
        ),
    )(
        flat(frames),
        flat(cache_first),
        flat(cache_second),
        gain_first,
        gain_second,
        bias_first,
        bias_second,
        flat(cotangent),
        shards,
    )
    return tuple(value.reshape(frames.shape) for value in outputs)


def local(n, groups, *arrays):
    frames, weight = arrays[0], arrays[7]
    fits = (
        n % 4 == 0
        and n >= 8
        and groups % 2 == 0
        and frames.shape[:2] == (2, 1)
        and frames.shape[2] % 16 == 0
        and frames.shape[3] % 128 == 0
        and weight.shape[1] % 8 == 0
    )
    if fits:
        return local_fused(n, groups, *arrays)
    return local_general(*arrays)


def solution(mesh):
    return jax.shard_map(
        functools.partial(local, mesh.shape["ha"], mesh.shape["grp"]),
        mesh=mesh,
        in_specs=(
            P("grp", "ha", None, None),
            P("grp", "ha", None, None),
            P("grp", "ha", None, None),
            P(),
            P(),
            P(),
            P(),
            P(None, "ha"),
            P(None, "ha"),
            P("grp", "ha", None, None),
        ),
        out_specs=(P("grp", "ha", None, None), P("grp", "ha", None, None)),
        check_vma=False,
    )
```

```python
import functools

import jax
import jax.numpy as jnp
from jax import lax
from jax.experimental import pallas as pl
from jax.experimental.pallas import tpu as pltpu
from jax.sharding import PartitionSpec as P


def extended_2(block, sides, width):
    for axis, dim in sides:
        count = lax.axis_size(axis)
        forward = [(i, i + 1) for i in range(count - 1)]
        backward = [(target, source) for source, target in forward]
        low = lax.ppermute(
            lax.slice_in_dim(block, block.shape[dim] - width, None, axis=dim), axis, forward
        )
        high = lax.ppermute(lax.slice_in_dim(block, 0, width, axis=dim), axis, backward)
        block = jnp.concatenate([low, block, high], axis=dim)
    return block


def normed_silu(values, scales):
    mean_square = jnp.mean(values * values, axis=-1, keepdims=True)
    inverse = lax.rsqrt(mean_square + 1e-06)
    normed = values * inverse * scales
    return normed * jax.nn.sigmoid(normed)


def silu_backward(values, scales, upstream):
    mean_square = jnp.mean(values * values, axis=-1, keepdims=True)
    inverse = lax.rsqrt(mean_square + 1e-06)
    normed = values * inverse * scales
    sigmoid_value = jax.nn.sigmoid(normed)
    scaled = scales * upstream * sigmoid_value * (1.0 + normed * (1.0 - sigmoid_value))
    return inverse * scaled - values * inverse**3 * jnp.mean(
        values * scaled, axis=-1, keepdims=True
    )


def tap_patches(padded, length, rows, columns, flipped):
    pieces = []
    for frame_tap in range(3):
        for row_tap in range(3):
            for col_tap in range(3):
                if flipped:
                    frame_start, row_start, col_start = (2 - frame_tap, 2 - row_tap, 2 - col_tap)
                else:
                    frame_start, row_start, col_start = (frame_tap, row_tap, col_tap)
                pieces.append(
                    padded[
                        frame_start : frame_start + length,
                        row_start : row_start + rows,
                        col_start : col_start + columns,
                    ]
                )
    return jnp.stack(pieces, axis=3)


def local_general(
    frames,
    cache_first,
    cache_second,
    gain_first,
    gain_second,
    bias_first,
    bias_second,
    weight_first,
    weight_second,
    cotangent,
):
    length, rows, columns, channels = frames.shape
    kernel_one, kernel_two = (
        lax.all_gather(weight_first, "ha", axis=1, tiled=True),
        lax.all_gather(weight_second, "ha", axis=1, tiled=True),
    )
    kernel_one = kernel_one.reshape(27, channels, channels)
    inputs = frames.astype(jnp.float32)
    first_act = normed_silu(inputs, gain_first).astype(jnp.bfloat16)
    extended = jnp.concatenate([cache_first, first_act], axis=0)
    padded = extended_2(extended, (("ha", 1),), 1)
    padded = jnp.pad(padded, ((0, 0), (0, 0), (1, 1), (0, 0)))
    patches = tap_patches(padded, length, rows, columns, False)
    middle = jnp.einsum("lrwtc,tco->lrwo", patches, kernel_one, preferred_element_type=jnp.float32)
    middle = (middle + bias_first).astype(jnp.bfloat16)
    middle_float = middle.astype(jnp.float32)
    kernel_two = kernel_two.reshape(27, channels, channels)
    second_act = normed_silu(middle_float, gain_second).astype(jnp.bfloat16)
    extended = jnp.concatenate([cache_second, second_act], axis=0)
    padded = extended_2(extended, (("ha", 1),), 1)
    padded = jnp.pad(padded, ((0, 0), (0, 0), (1, 1), (0, 0)))
    patches = tap_patches(padded, length, rows, columns, False)
    second_out = jnp.einsum(
        "lrwtc,tco->lrwo", patches, kernel_two, preferred_element_type=jnp.float32
    )
    output = (inputs + second_out + bias_second).astype(jnp.bfloat16)
    padded = extended_2(cotangent, (("ha", 1),), 1)
    padded = jnp.pad(padded, ((0, 2), (0, 0), (1, 1), (0, 0)))
    patches = tap_patches(padded, length, rows, columns, True)
    grad_second = jnp.einsum(
        "lrwto,tco->lrwc", patches, kernel_two, preferred_element_type=jnp.float32
    )
    grad_middle = silu_backward(middle_float, gain_second, grad_second).astype(jnp.bfloat16)
    padded = extended_2(grad_middle, (("ha", 1),), 1)
    padded = jnp.pad(padded, ((0, 2), (0, 0), (1, 1), (0, 0)))
    patches = tap_patches(padded, length, rows, columns, True)
    grad_first = jnp.einsum(
        "lrwto,tco->lrwc", patches, kernel_one, preferred_element_type=jnp.float32
    )
    grad_frames = (
        cotangent.astype(jnp.float32) + silu_backward(inputs, gain_first, grad_first)
    ).astype(jnp.bfloat16)
    return (output, grad_frames)


MESH = pl.DeviceIdType.MESH
DEPTH = 2
LINE_AHEAD = 3 * DEPTH


def block_kernel(
    n,
    groups,
    columns,
    frames_ref,
    cache_first_ref,
    cache_second_ref,
    gain_first_ref,
    gain_second_ref,
    bias_first_ref,
    bias_second_ref,
    cotangent_ref,
    shards,
    output_ref,
    grad_ref,
    buf,
    weights,
    early,
    act,
    grad_mid,
    patches_one,
    patches_two,
    acc,
    acc_t,
    middle_ref,
    z_send,
    z_recv,
    y_send,
    y_recv,
    x_send,
    x_recv,
    s_send,
    s_recv,
    t_send,
    t_recv,
    halo_send,
    halo_recv,
    local_sem,
):
    f32, bf16 = jnp.float32, jnp.bfloat16
    chunks, tiles, width, _ = shards.shape
    half = chunks // 2
    lanes = tiles * 128
    channels = lanes // 3
    give = tiles // 2
    own = tiles - give
    two = 2 * columns
    length = n // 4
    me = lax.axis_index("ha")
    group = lax.axis_index("grp")
    core = lax.rem(me, 2)
    row = lax.rem(me // 2, 2)
    line = me // 4
    odd = lax.rem(group, 2)
    own_part = pl.ds(odd * give, own)
    give_part = pl.ds(odd * own, give)
    take_part = pl.ds((1 - odd) * own, give)

    def at(line_, row_, core_):
        return {"ha": (line_ * 2 + row_) * 2 + core_}

    sibling = at(line, row, 1 - core)
    across = at(line, 1 - row, core)
    twin = {"grp": group + 1 - 2 * odd}

    def line_peer(step):
        return at(lax.rem(line + step, length), row, core)

    barrier = pltpu.get_barrier_semaphore()
    partners = [sibling, across, twin] + [line_peer(s) for s in range(1, length)]
    for partner in partners:
        pl.semaphore_signal(barrier, inc=1, device_id=partner, device_id_type=MESH)

    has_low, has_high = me > 0, me < n - 1

    @pl.when(has_low)
    def _():
        pl.semaphore_signal(barrier, inc=1, device_id={"ha": me - 1}, device_id_type=MESH)

    @pl.when(has_high)
    def _():
        pl.semaphore_signal(barrier, inc=1, device_id={"ha": me + 1}, device_id_type=MESH)

    keep = pltpu.make_async_copy(
        shards,
        buf.at[:, core, row, line],
        local_sem,
    )
    keep.start()
    pl.semaphore_wait(
        barrier, len(partners) + has_low.astype(jnp.int32) + has_high.astype(jnp.int32)
    )

    def remote(src, dst, send, recv, device):
        return pltpu.make_async_remote_copy(
            src_ref=src, dst_ref=dst, send_sem=send, recv_sem=recv, device_id=device, device_id_type=MESH
        )

    def z_copy(q, step, source):
        return remote(
            shards.at[q, own_part],
            buf.at[q, core, row, source, own_part],
            z_send.at[q, step - 1],
            z_recv.at[q, step - 1],
            line_peer(step),
        )

    def same(view, send, recv, device):
        return remote(view, view, send, recv, device)

    def y_copy(q, row_):
        view = buf.at[q, core, row_, :, own_part]
        return same(view, y_send.at[q], y_recv.at[q], across)

    def x_one(q, step, part):
        source = lax.rem(line - step + length, length)
        view = buf.at[q, core, row, source, part]
        return same(view, x_send.at[q, step - 1], x_recv.at[q, step - 1], twin)

    def x_rest(q, part):
        view = buf.at[q, core, 1 - row, :, part]
        return same(view, x_send.at[q, length - 1], x_recv.at[q, length - 1], twin)

    def s_copy(q, core_):
        view = buf.at[q, core_, :, :, own_part]
        return same(view, s_send.at[q], s_recv.at[q], sibling)

    def t_copy(q, core_):
        view = buf.at[q, core_, :, :, take_part]
        return same(view, t_send.at[q], t_recv.at[q], sibling)

    def z_start(q):
        for step in range(1, length):
            z_copy(q, step, line).start()

    def halo_copies(ref, index):
        low = remote(
            ref.at[1], ref.at[2], halo_send.at[index, 0], halo_recv.at[index, 0], {"ha": me - 1}
        )
        high = remote(
            ref.at[1], ref.at[0], halo_send.at[index, 1], halo_recv.at[index, 1], {"ha": me + 1}
        )
        return low, high

    def halo_start(ref, index):
        low, high = halo_copies(ref, index)

        @pl.when(has_low)
        def _():
            low.start()

        @pl.when(has_high)
        def _():
            high.start()

    def halo_wait(ref, index):
        low, high = halo_copies(ref, index)

        @pl.when(has_low)
        def _():
            high.wait_recv()
            low.wait_send()

        @pl.when(has_high)
        def _():
            low.wait_recv()
            high.wait_send()

        @pl.when(jnp.logical_not(has_low))
        def _():
            ref[0] = jnp.zeros(ref.shape[1:], ref.dtype)

        @pl.when(jnp.logical_not(has_high))
        def _():
            ref[2] = jnp.zeros(ref.shape[1:], ref.dtype)

    def comm(t):
        q = t + LINE_AHEAD + 4

        @pl.when(q < chunks)
        def _():
            z_start(q)

        q_z = t + LINE_AHEAD

        @pl.when(q_z < chunks)
        def _():
            for step in range(1, length):
                z_copy(q_z, step, lax.rem(line - step + length, length)).wait_recv()
            y_copy(q_z, row).start()
            for step in range(1, length):
                x_one(q_z, step, give_part).start()

        q_y = t + 2 * DEPTH

        @pl.when(jnp.logical_and(q_y >= 0, q_y < chunks))
        def _():
            y_copy(q_y, 1 - row).wait_recv()
            x_rest(q_y, give_part).start()
            s_copy(q_y, core).start()

        q_x = t + DEPTH

        @pl.when(jnp.logical_and(q_x >= 0, q_x < chunks))
        def _():
            for step in range(1, length):
                x_one(q_x, step, take_part).wait_recv()
            x_rest(q_x, take_part).wait_recv()
            t_copy(q_x, core).start()

        @pl.when(t >= 0)
        def _():
            s_copy(t, 1 - core).wait_recv()
            t_copy(t, 1 - core).wait_recv()
            for index in range(n):
                rows = slice(index * width, (index + 1) * width)
                for m in range(tiles):
                    weights[t, rows, m * 128 : (m + 1) * 128] = buf[
                        t, index % 2, index // 2 % 2, index // 4, m
                    ]

    def column(shape):
        return lax.rem(lax.broadcasted_iota(jnp.int32, shape, 0), columns)

    def shifted(value, by):
        rolled = pltpu.roll(value, by % value.shape[0], 0)
        edge = 0 if by > 0 else columns - 1
        return jnp.where(column(value.shape) == edge, 0.0, rolled)

    def unfold(src, src_start, dst, dst_start, count):
        for j in range(3):
            value = src[j, src_start : src_start + count, :]
            wide = value.astype(f32)
            rows = slice(dst_start, dst_start + count)
            dst[j, rows, :channels] = shifted(wide, 1).astype(bf16)
            dst[j, rows, channels : 2 * channels] = value
            dst[j, rows, 2 * channels :] = shifted(wide, -1).astype(bf16)

    def forward_dot(patches, q, i, j):
        window = patches[j, pl.ds(pl.multiple_of(i * columns, 16), two), :]
        acc[...] += lax.dot_general(
            weights[q], window, (((1,), (1,)), ((), ())), preferred_element_type=f32
        )

    def back_late(ref, start, q, j):
        acc_t[...] += jnp.dot(
            ref[2 - j, start : start + two, :], weights[q], preferred_element_type=f32
        )

    def back_early(ref, start, q, j):
        acc_t[:columns, :] += jnp.dot(
            ref[2 - j, start + columns : start + two, :], weights[q], preferred_element_type=f32
        )

    def folded():
        return (
            shifted(acc_t[:, :channels], -1)
            + acc_t[:, channels : 2 * channels]
            + shifted(acc_t[:, 2 * channels :], 1)
        )

    for q in range(min(4, chunks)):
        z_start(q)

    early[1, :two, :] = cache_first_ref[...]
    early[1, two : 2 * two, :] = normed_silu(frames_ref[...].astype(f32), gain_first_ref[...].reshape(1, channels)).astype(bf16)
    early[1, 2 * two : 3 * two, :] = cache_second_ref[...]
    early[1, 3 * two :, :] = cotangent_ref[...]
    halo_start(early, 0)
    keep.wait()

    @pl.loop(-LINE_AHEAD, -DEPTH)
    def _(t):
        comm(t)

    halo_wait(early, 0)
    unfold(early, 0, patches_one, 0, 2 * two)
    unfold(early, 2 * two, patches_two, 0, two)

    @pl.loop(-DEPTH, 0)
    def _(t):
        comm(t)

    acc[...] = jnp.zeros(acc.shape, f32)

    @pl.loop(0, half)
    def _(t):
        comm(t)
        forward_dot(patches_one, t, t // 3, lax.rem(t, 3))

    middle_ref[...] = (acc[...].T + bias_first_ref[...].reshape(1, channels)).astype(bf16)
    act[1] = normed_silu(middle_ref[...].astype(f32), gain_second_ref[...].reshape(1, channels)).astype(bf16)
    halo_start(act, 1)
    acc[...] = jnp.zeros(acc.shape, f32)
    acc_t[...] = jnp.zeros(acc_t.shape, f32)

    @pl.loop(0, 3)
    def _(j):
        comm(half + j)
        back_late(early, 3 * two, half + j, j)

    halo_wait(act, 1)
    unfold(act, 0, patches_two, two, two)

    @pl.loop(0, 3)
    def _(j):
        comm(half + 3 + j)
        back_early(early, 3 * two, half + 3 + j, j)
        forward_dot(patches_two, half + j, 2, j)
        forward_dot(patches_two, half + 3 + j, 1, j)

    grad_mid[1] = silu_backward(
        middle_ref[...].astype(f32), gain_second_ref[...].reshape(1, channels), folded()
    ).astype(bf16)
    halo_start(grad_mid, 2)
    acc_t[...] = jnp.zeros(acc_t.shape, f32)

    @pl.loop(0, 2)
    def _(j):
        comm(half + 6 + j)
        forward_dot(patches_two, half + 6 + j, 0, j)

    halo_wait(grad_mid, 2)

    @pl.loop(0, 3)
    def _(j):
        back_late(grad_mid, 0, 6 + j, j)
        back_early(grad_mid, 0, 3 + j, j)

    comm(half + 8)
    forward_dot(patches_two, half + 8, 0, 2)

    inputs = frames_ref[...].astype(f32)
    output_ref[...] = (inputs + acc[...].T + bias_second_ref[...].reshape(1, channels)).astype(bf16)
    grad_ref[...] = (
        cotangent_ref[...].astype(f32) + silu_backward(inputs, gain_first_ref[...].reshape(1, channels), folded())
    ).astype(bf16)

    @pl.loop(0, chunks)
    def _(q):
        for step in range(1, length):
            z_copy(q, step, line).wait_send()
            x_one(q, step, give_part).wait_send()
        y_copy(q, row).wait_send()
        x_rest(q, give_part).wait_send()
        s_copy(q, core).wait_send()
        t_copy(q, core).wait_send()


def local_fused(
    n,
    groups,
    frames,
    cache_first,
    cache_second,
    gain_first,
    gain_second,
    bias_first,
    bias_second,
    weight_first,
    weight_second,
    cotangent,
):
    _, _, columns, channels = frames.shape
    rows, width = weight_first.shape
    f32, bf16 = jnp.float32, jnp.bfloat16
    lanes = 3 * channels
    two = 2 * columns
    tiles = lanes // 128
    one = weight_first.T.reshape(width, 9, tiles, 128).transpose(1, 2, 0, 3)
    other = weight_second.T.reshape(width, 9, tiles, 128).transpose(1, 2, 0, 3)
    shards = jnp.concatenate([one, other[6:], other[3:6], other[:3]], axis=0)
    flat = lambda value: value.reshape(two, channels)
    vmem = pl.BlockSpec(memory_space=pltpu.VMEM)
    dma = pltpu.SemaphoreType.DMA
    chunks, length = 18, n // 4
    outputs = pl.pallas_call(
        functools.partial(block_kernel, n, groups, columns),
        out_shape=[jax.ShapeDtypeStruct((two, channels), bf16)] * 2,
        in_specs=[vmem] * 9,
        out_specs=[vmem] * 2,
        scratch_shapes=[
            pltpu.VMEM((chunks, 2, 2, length, tiles, width, 128), bf16),
            pltpu.VMEM((chunks, channels, lanes), bf16),
            pltpu.VMEM((3, 4 * two, channels), bf16),
            pltpu.VMEM((3, two, channels), bf16),
            pltpu.VMEM((3, two, channels), bf16),
            pltpu.VMEM((3, 2 * two, lanes), bf16),
            pltpu.VMEM((3, 2 * two, lanes), bf16),
            pltpu.VMEM((channels, two), f32),
            pltpu.VMEM((two, lanes), f32),
            pltpu.VMEM((two, channels), bf16),
            dma((chunks, length - 1)),
            dma((chunks, length - 1)),
            dma((chunks,)),
            dma((chunks,)),
            dma((chunks, length)),
            dma((chunks, length)),
            dma((chunks,)),
            dma((chunks,)),
            dma((chunks,)),
            dma((chunks,)),
            dma((3, 2)),
            dma((3, 2)),
            dma,
        ],
        compiler_params=pltpu.CompilerParams(
            collective_id=0, has_side_effects=True, vmem_limit_bytes=60 * 1024 * 1024
        ),
        cost_estimate=pl.CostEstimate(
            flops=6 * two * rows * channels, bytes_accessed=8 * rows * width, transcendentals=0
        ),
    )(
        flat(frames),
        flat(cache_first),
        flat(cache_second),
        gain_first,
        gain_second,
        bias_first,
        bias_second,
        flat(cotangent),
        shards,
    )
    return tuple(value.reshape(frames.shape) for value in outputs)


def local(n, groups, *arrays):
    frames, weight = arrays[0], arrays[7]
    fits = (
        n % 4 == 0
        and n >= 8
        and groups % 2 == 0
        and frames.shape[:2] == (2, 1)
        and frames.shape[2] % 16 == 0
        and frames.shape[3] % 128 == 0
        and weight.shape[1] % 8 == 0
    )
    if fits:
        return local_fused(n, groups, *arrays)
    return local_general(*arrays)


def solution(mesh):
    return jax.shard_map(
        functools.partial(local, mesh.shape["ha"], mesh.shape["grp"]),
        mesh=mesh,
        in_specs=(
            P("grp", "ha", None, None),
            P("grp", "ha", None, None),
            P("grp", "ha", None, None),
            P(),
            P(),
            P(),
            P(),
            P(None, "ha"),
            P(None, "ha"),
            P("grp", "ha", None, None),
        ),
        out_specs=(P("grp", "ha", None, None), P("grp", "ha", None, None)),
        check_vma=False,
    )
```
